512 devices in a mesh: param: 32 (over z, core), ex: 16 (over y, x).
Axes of the slice: x: 4, y: 4, z: 16, core: 2. Of those that a mesh axis runs over, the one named last changes fastest.
Arguments:
- activations: bfloat16 [32, 1024, 4096], P('ex', None, 'param'), may hold values from -6 to 6
- out_grad: bfloat16 [32, 1024, 4096], P('ex', 'param'), may hold values from -6 to 6
- sign_bits: int32 [4096, 4096], P('param'), may hold values from 0 to 1
- sample_index: int32 [8192], replicated, may hold values from 0 to 16777215, as said below
Outputs:
- features: float32 [32, 8192], P('ex', 'param')
- gram: float32 [32, 32], P('ex')
The draws below stay inside these ranges and needn't reach their ends.
Inputs may be any that keep to these rules, and one draw needn't show every extreme that they name: `sample_index`: feature k samples a coordinate of the k // 256-th of the 32 consecutive blocks of 524288 coordinates.
All inputs are finite; a program needn't handle non-finite values.
Results may differ from the reference program's by a relative error of at most 0.0003.
Values may be sent and summed in bfloat16 or wider, within the bound.
No kernel may reach another device: no remote copies, remote signals or barrier semaphores. Data moves between devices by JAX's collectives and lax.ppermute only.
A program may use at most 64 MiB of HBM per device.

```python
import jax
import jax.numpy as jnp
import numpy as np
from jax import lax

D = 4096
K = 8192
SEQ = 1024
EXAMPLES = 32
N_PARAM = 32


def draw_sample_index(key, part):
    key = jax.random.fold_in(key, 7)
    per = K // N_PARAM
    block = D * D // N_PARAM
    first, second, third = jax.random.split(key, 3)
    offsets = jax.random.randint(first, (K,), 0, block, dtype=jnp.int32)
    lead = jax.random.randint(second, (), 0, per, dtype=jnp.int32)
    tail = jax.random.randint(third, (), K - per, K, dtype=jnp.int32)
    position = jnp.arange(K, dtype=jnp.int32)
    offsets = jnp.where(position == lead, 0, offsets)
    offsets = jnp.where(position == tail, block - 1, offsets)
    return (position // per * block + offsets).astype(jnp.int32)


def with_ends(values, rng, smallest, high):
    dims = values.shape
    spot = [jax.random.randint(jax.random.fold_in(rng, axis), (), 0, dims[axis]) for axis in range(len(dims))]
    values = values.at[tuple(spot)].set(smallest)
    longest = dims.index(max(dims))
    spot[longest] = (spot[longest] + 1) % dims[longest]
    return values.at[tuple(spot)].set(high)


def shard_levels(stream_key, extent, cuts, least, top_value):
    level = 1.0
    for dim, shards_of in cuts:
        draws = jax.random.uniform(jax.random.fold_in(jax.random.fold_in(stream_key, 6), dim), (shards_of,), jnp.float32, least / len(cuts), top_value / len(cuts))
        level = level * jnp.repeat(jnp.exp(draws), extent[dim] // shards_of).reshape((-1,) + (1,) * (len(extent) - 1 - dim))
    return level


def noise(stream_key, shape, spread, limit, cuts=(), kind=jnp.bfloat16):
    entries = spread * jax.random.normal(stream_key, shape, jnp.float32)
    if cuts:
        entries = entries * shard_levels(stream_key, shape, cuts, -0.22, 0.18)
    return jnp.clip(entries, -limit, limit).astype(kind)


def setup_inputs(seed: int = 0) -> dict:
    seeds = jax.random.split(jax.random.key(seed), 5)
    return {
        "activations": noise(seeds[0], (EXAMPLES, SEQ, D), 1.0, 6.0, ((0, 16), (2, 32))),
        "out_grad": noise(seeds[1], (EXAMPLES, SEQ, D), 1.0, 6.0, ((0, 16), (1, 32))),
        "sign_bits": with_ends(jax.random.randint(seeds[2], (D, D), 0, 2), jax.random.fold_in(seeds[2], 1), 0, 1).astype(jnp.int32),
        "sample_index": draw_sample_index(jax.random.fold_in(seeds[4], 71), 0),
    }


def sylvester(order):
    table = np.ones((1, 1), np.float32)
    base = np.array([[1.0, 1.0], [1.0, -1.0]], np.float32)
    while table.shape[0] < order:
        table = np.kron(table, base)
    return table

def transform(signed):
    width = signed.shape[0]
    inner = min(width, 128)
    outer = width // inner
    small = jnp.asarray(sylvester(inner), jnp.float32)
    large = jnp.asarray(sylvester(outer), jnp.float32)
    hp = lax.Precision.HIGHEST
    cube = signed.reshape(outer, inner, outer, inner)
    cube = jnp.einsum('abcd,de->abce', cube, small, precision=hp)
    cube = jnp.einsum('abcd,ce->abed', cube, large, precision=hp)
    cube = jnp.einsum('abcd,be->aecd', cube, small, precision=hp)
    cube = jnp.einsum('abcd,ae->ebcd', cube, large, precision=hp)
    return cube.reshape(-1)

def reference(activations, out_grad, sign_bits, sample_index):
    scale = 1.0 / (D * math_sqrt(SEQ))

    def one_example(pair):
        act, grd = pair
        grad = jnp.dot(act.T, grd, preferred_element_type=jnp.float32)
        signed = jnp.where(sign_bits == 1, grad, -grad)
        mixed = transform(signed)
        return jnp.take(mixed, sample_index, axis=0) * scale
    features = lax.map(one_example, (activations, out_grad))
    gram = jnp.dot(features, features.T, precision=lax.Precision.HIGHEST) / K
    return (features, gram)

def math_sqrt(value):
    return float(value) ** 0.5
```

```python
import jax
import jax.numpy as jnp
import numpy as np
from jax import lax
from jax.experimental import pallas as pl
from jax.experimental.pallas import tpu as pltpu
from jax.sharding import PartitionSpec as P

LANES = 128


def sylvester(order):
    table = np.ones((1, 1), np.float32)
    base = np.array([[1.0, 1.0], [1.0, -1.0]], np.float32)
    while table.shape[0] < order:
        table = np.kron(table, base)
    return table


def halves(value):
    high = value.astype(jnp.bfloat16)
    low = (value - high.astype(jnp.float32)).astype(jnp.bfloat16)
    return high, low


def sampled_transform(rows_ref, grad_ref, bits_ref, pattern_ref, table_ref, ones_ref, out_ref, mixed, stage):
    examples, rows, width = grad_ref.shape
    outer = width // LANES
    wide = 4 * LANES
    pieces = width // wide

    def row_step(i, carry):
        example, piece = lax.div(i, pieces), lax.rem(i, pieces)
        columns = pl.ds(pl.multiple_of(piece * wide, wide), wide)
        value = grad_ref[example, :, columns]
        signed = jnp.where(bits_ref[:, columns] == 1, value, -value)
        out = jnp.dot(table_ref[...], jnp.concatenate(halves(signed), axis=0), preferred_element_type=jnp.float32)
        for t in range(wide // LANES):
            first = pl.multiple_of((piece * (wide // LANES) + t) * rows, rows)
            mixed[example, pl.ds(first, rows), :] = out[:, t * LANES:(t + 1) * LANES]
        return carry

    lax.fori_loop(0, examples * pieces, row_step, 0)

    def outer_step(i, carry):
        example, first = lax.div(i, rows // 8), pl.multiple_of(lax.rem(i, rows // 8) * 8, 8)
        tiles = [mixed[example, pl.ds(pl.multiple_of(m * rows + first, 8), 8), :] for m in range(outer)]
        step = 1
        while step < outer:
            tiles = [tiles[m ^ step] - tiles[m] if m & step else tiles[m] + tiles[m ^ step] for m in range(outer)]
            step *= 2
        for m in range(outer):
            mixed[example, pl.ds(pl.multiple_of(m * rows + first, 8), 8), :] = tiles[m]
        return carry

    lax.fori_loop(0, examples * (rows // 8), outer_step, 0)

    diagonal = lax.broadcasted_iota(jnp.int32, (LANES, LANES), 0) == lax.broadcasted_iota(jnp.int32, (LANES, LANES), 1)

    def sample_step(i, carry):
        for s in range(LANES):
            row = rows_ref[i * LANES + s]
            for example in range(examples):
                stage[example, pl.ds(s, 1), :] = mixed[example, pl.ds(row, 1), :]
        pattern = pattern_ref[pl.ds(pl.multiple_of(i * LANES, LANES), LANES), :].astype(jnp.float32)
        for example in range(examples):
            terms = jnp.concatenate(halves(stage[example] * pattern), axis=1)
            total = jnp.dot(terms, ones_ref[...], preferred_element_type=jnp.float32)
            out_ref[example, pl.ds(i, 1), :] = jnp.sum(jnp.where(diagonal, total, 0.0), axis=0, keepdims=True)
        return carry

    lax.fori_loop(0, out_ref.shape[1], sample_step, 0)


def local_samples(grad, sign_bits, sample_index):
    examples, rows, width = grad.shape
    count = sample_index.shape[0]
    local = sample_index % (rows * width)
    row, column = local // width, local % width
    where_row = column // LANES * rows + row
    inner = (column % LANES)[:, None] == jnp.arange(LANES, dtype=jnp.int32)[None]
    small = jnp.asarray(sylvester(LANES), jnp.bfloat16)
    pattern = jnp.dot(inner.astype(jnp.bfloat16), small, preferred_element_type=jnp.float32).astype(jnp.bfloat16)
    table = jnp.asarray(np.concatenate([sylvester(rows)] * 2, axis=1), jnp.bfloat16)
    ones = jnp.ones((2 * LANES, LANES), jnp.bfloat16)
    vmem = pl.BlockSpec(memory_space=pltpu.VMEM)
    out = pl.pallas_call(
        sampled_transform,
        out_shape=jax.ShapeDtypeStruct((examples, count // LANES, LANES), jnp.float32),
        in_specs=[pl.BlockSpec(memory_space=pltpu.SMEM)] + [vmem] * 5,
        out_specs=vmem,
        scratch_shapes=[
            pltpu.VMEM((examples, rows * width // LANES, LANES), jnp.float32),
            pltpu.VMEM((examples, LANES, LANES), jnp.float32),
        ],
        compiler_params=pltpu.CompilerParams(vmem_limit_bytes=40 * 1024 * 1024),
        name="sampled_transform",
    )(where_row, grad, sign_bits, pattern, table, ones)
    return out.reshape(examples, count)


def per_device(activations, out_grad, sign_bits, sample_index):
    count, seq_len, rows = activations.shape
    width = out_grad.shape[2]
    devices = lax.axis_size("param")
    me = lax.axis_index("param")
    gathered = lax.all_gather(out_grad, "param", axis=1, tiled=True)
    grad = jnp.einsum("etr,etd->erd", activations, gathered, preferred_element_type=jnp.float32)
    picked = local_samples(grad, sign_bits, sample_index)
    feature_count = picked.shape[1]
    per = feature_count // devices
    grouped = picked.reshape(count, devices, per).transpose(1, 0, 2)
    terms = lax.all_to_all(grouped, "param", 0, 0, tiled=True)
    table = jnp.asarray(sylvester(devices), jnp.float32)
    column = lax.dynamic_slice_in_dim(table, me, 1, 0)[0]
    scale = 1.0 / (width * float(seq_len) ** 0.5)
    features = jnp.sum(terms * column[:, None, None], axis=0) * scale
    everyone = lax.all_gather(features, "ex", axis=0, tiled=True)
    inner = jnp.dot(features, everyone.T, precision=lax.Precision.HIGHEST)
    gram = jnp.sum(lax.all_gather(inner, "param", axis=0), axis=0) / feature_count
    return (features, gram)


def solution(mesh):
    return jax.shard_map(
        per_device,
        mesh=mesh,
        in_specs=(P("ex", None, "param"), P("ex", "param", None), P("param", None), P()),
        out_specs=(P("ex", "param"), P("ex", None)),
        check_vma=False,
    )
```

```python
import jax
import jax.numpy as jnp
import numpy as np
from jax import lax
from jax.experimental import pallas as pl
from jax.experimental.pallas import tpu as pltpu
from jax.sharding import Mesh, PartitionSpec as P

LANES = 128
WIDE = 512


def sylvester(order):
    table = np.ones((1, 1), np.float32)
    base = np.array([[1.0, 1.0], [1.0, -1.0]], np.float32)
    while table.shape[0] < order:
        table = np.kron(table, base)
    return table


def halves(value):
    high = value.astype(jnp.bfloat16)
    low = (value - high.astype(jnp.float32)).astype(jnp.bfloat16)
    return high, low


def sampled_gradient(rows_ref, act_ref, grd_ref, near_ref, far_ref, pattern_ref, table_ref, ones_ref, out_ref, mixed, stage):
    rows = act_ref.shape[0]
    outer = mixed.shape[0] // rows
    piece = pl.program_id(0)

    value = jnp.dot(act_ref[...], grd_ref[...], preferred_element_type=jnp.float32)
    near, far = value[: rows // 2], value[rows // 2:]
    near = jnp.where(near_ref[...] == 1, near, -near)
    far = jnp.where(far_ref[...] == 1, far, -far)
    parts = [part for half in zip(halves(near), halves(far)) for part in half]
    out = jnp.dot(table_ref[...], jnp.concatenate(parts, axis=0), preferred_element_type=jnp.float32)
    for t in range(WIDE // LANES):
        first = pl.multiple_of((piece * (WIDE // LANES) + t) * rows, rows)
        mixed[pl.ds(first, rows), :] = out[:, t * LANES:(t + 1) * LANES]

    @pl.when(piece == pl.num_programs(0) - 1)
    def _():
        def outer_step(i, carry):
            first = pl.multiple_of(i * 8, 8)
            tiles = [mixed[pl.ds(pl.multiple_of(m * rows + first, 8), 8), :] for m in range(outer)]
            step = 1
            while step < outer:
                tiles = [tiles[m ^ step] - tiles[m] if m & step else tiles[m] + tiles[m ^ step] for m in range(outer)]
                step *= 2
            for m in range(outer):
                mixed[pl.ds(pl.multiple_of(m * rows + first, 8), 8), :] = tiles[m]
            return carry

        lax.fori_loop(0, rows // 8, outer_step, 0)

        diagonal = lax.broadcasted_iota(jnp.int32, (LANES, LANES), 0) == lax.broadcasted_iota(jnp.int32, (LANES, LANES), 1)

        def sample_step(i, carry):
            for s in range(LANES):
                stage[pl.ds(s, 1), :] = mixed[pl.ds(rows_ref[i * LANES + s], 1), :]
            pattern = pattern_ref[pl.ds(pl.multiple_of(i * LANES, LANES), LANES), :].astype(jnp.float32)
            terms = jnp.concatenate(halves(stage[...] * pattern), axis=1)
            total = jnp.dot(terms, ones_ref[...], preferred_element_type=jnp.float32)
            out_ref[pl.ds(i, 1), :] = jnp.sum(jnp.where(diagonal, total, 0.0), axis=0, keepdims=True)
            return carry

        lax.fori_loop(0, out_ref.shape[0], sample_step, 0)


def local_samples(act, grd, near, far, core, sample_index):
    rows, tokens = act.shape
    width = grd.shape[1]
    count = sample_index.shape[0]
    local = sample_index % (rows * width)
    row, column = local // width, local % width
    where_row = column // LANES * rows + row
    inner = (column % LANES)[:, None] == jnp.arange(LANES, dtype=jnp.int32)[None]
    small = jnp.asarray(sylvester(LANES), jnp.bfloat16)
    pattern = jnp.dot(inner.astype(jnp.bfloat16), small, preferred_element_type=jnp.float32).astype(jnp.bfloat16)
    full = sylvester(rows)
    left, right = full[:, : rows // 2], full[:, rows // 2:]
    tables = np.stack([np.concatenate(pair, axis=1) for pair in ((left, right, left, right), (right, left, right, left))])
    table = lax.dynamic_index_in_dim(jnp.asarray(tables, jnp.bfloat16), core, 0, keepdims=False)
    ones = jnp.ones((2 * LANES, LANES), jnp.bfloat16)
    whole = lambda *shape: pl.BlockSpec(shape, lambda i: (0,) * len(shape))
    columns = lambda depth: pl.BlockSpec((depth, WIDE), lambda i: (0, i))
    out = pl.pallas_call(
        sampled_gradient,
        grid=(width // WIDE,),
        out_shape=jax.ShapeDtypeStruct((count // LANES, LANES), jnp.float32),
        in_specs=[
            pl.BlockSpec(memory_space=pltpu.SMEM),
            whole(rows, tokens),
            columns(tokens),
            columns(rows // 2),
            columns(rows // 2),
            whole(count, LANES),
            whole(rows, 2 * rows),
            whole(2 * LANES, LANES),
        ],
        out_specs=whole(count // LANES, LANES),
        scratch_shapes=[
            pltpu.VMEM((rows * width // LANES, LANES), jnp.float32),
            pltpu.VMEM((LANES, LANES), jnp.float32),
        ],
        compiler_params=pltpu.CompilerParams(vmem_limit_bytes=40 * 1024 * 1024),
        name="sampled_gradient",
    )(where_row, act, grd, near, far, pattern, table, ones)
    return out


def to_all(value, axes):
    size = lax.axis_size(axes)
    return lax.all_to_all(jnp.broadcast_to(value[None], (size,) + value.shape), axes, 0, 0, tiled=True)


def per_device(activations, out_grad, sign_bits, sample_index):
    count, seq_len, columns = activations.shape
    width = out_grad.shape[2]
    chips = lax.axis_size("z")
    here, core = lax.axis_index("z"), lax.axis_index("core")
    swap = [(0, 1), (1, 0)]

    mine = lambda pair: lax.dynamic_index_in_dim(pair, core, 0, keepdims=False)
    other = lambda pair: lax.ppermute(lax.dynamic_index_in_dim(pair, 1 - core, 0, keepdims=False), "core", swap)
    block = jnp.concatenate([mine(out_grad), other(out_grad)], axis=0)
    gathered = lax.all_gather(block, "z", axis=0, tiled=True)
    far = lax.ppermute(sign_bits, "core", swap)
    act = jnp.concatenate([mine(activations), other(activations)], axis=1).T
    act = act.reshape(2 * columns, chips, 2, seq_len // (2 * chips))
    act = jnp.where(core == 0, act, act[:, :, ::-1]).reshape(2 * columns, seq_len)

    terms = local_samples(act, gathered, sign_bits, far, core, sample_index)
    feature_count = sample_index.shape[0]
    per = feature_count // (2 * chips)
    terms = lax.all_to_all(terms.reshape(2 * chips, per), ("z", "core"), 0, 0, tiled=True)
    signs = lax.dynamic_index_in_dim(jnp.asarray(sylvester(chips), jnp.float32), here, 0, keepdims=False)
    scale = 1.0 / (width * float(seq_len) ** 0.5)
    features = jnp.sum(terms.reshape(chips, 2, per) * signs[:, None, None], axis=0) * scale
    everyone = to_all(features, "ex").reshape(-1, per)
    inner = jnp.dot(features, everyone.T, precision=lax.Precision.HIGHEST)
    gram = jnp.sum(to_all(inner, ("z", "core")), axis=0) / feature_count
    return (features, gram)


def solution(mesh):
    params, groups = mesh.devices.shape
    chips = Mesh(mesh.devices.reshape(params // 2, 2, groups), ("z", "core", "ex"))
    param = ("z", "core")
    return jax.shard_map(
        per_device,
        mesh=chips,
        in_specs=(P("ex", None, param), P("ex", param, None), P(param, None), P()),
        out_specs=(P("ex", param), P("ex", None)),
        check_vma=False,
    )
```

```python
import jax
import jax.numpy as jnp
import numpy as np
from jax import lax
from jax.experimental import pallas as pl
from jax.experimental.pallas import tpu as pltpu
from jax.sharding import Mesh, PartitionSpec as P

LANES = 128
WIDE = 1024
BATCH = 1024


def sylvester(order):
    table = np.ones((1, 1), np.float32)
    base = np.array([[1.0, 1.0], [1.0, -1.0]], np.float32)
    while table.shape[0] < order:
        table = np.kron(table, base)
    return table


def halves(value):
    high = value.astype(jnp.bfloat16)
    low = (value - high.astype(jnp.float32)).astype(jnp.bfloat16)
    return high, low


def sampled_gradient(rows_ref, act_ref, grd_ref, near_ref, far_ref, pattern_ref, table_ref, ones_ref, out_ref, mixed, stage):
    rows = act_ref.shape[0]
    outer = mixed.shape[0] // rows
    piece = pl.program_id(0)

    value = jnp.dot(act_ref[...], grd_ref[...], preferred_element_type=jnp.float32)
    near, far = value[: rows // 2], value[rows // 2:]
    columns = pl.ds(pl.multiple_of(piece * WIDE, WIDE), WIDE)
    near = jnp.where(near_ref[:, columns] == 1, near, -near)
    far = jnp.where(far_ref[:, columns] == 1, far, -far)
    parts = [part for half in zip(halves(near), halves(far)) for part in half]
    out = jnp.dot(table_ref[...], jnp.concatenate(parts, axis=0), preferred_element_type=jnp.float32)
    for t in range(WIDE // LANES):
        first = pl.multiple_of((piece * (WIDE // LANES) + t) * rows, rows)
        mixed[pl.ds(first, rows), :] = out[:, t * LANES:(t + 1) * LANES]

    @pl.when(piece == pl.num_programs(0) - 1)
    def _():
        def outer_step(i, carry):
            first = pl.multiple_of(i * 8, 8)
            tiles = [mixed[pl.ds(pl.multiple_of(m * rows + first, 8), 8), :] for m in range(outer)]
            step = 1
            while step < outer:
                tiles = [tiles[m ^ step] - tiles[m] if m & step else tiles[m] + tiles[m ^ step] for m in range(outer)]
                step *= 2
            for m in range(outer):
                mixed[pl.ds(pl.multiple_of(m * rows + first, 8), 8), :] = tiles[m]
            return carry

        lax.fori_loop(0, rows // 8, outer_step, 0)

        diagonal = lax.broadcasted_iota(jnp.int32, (LANES, LANES), 0) == lax.broadcasted_iota(jnp.int32, (LANES, LANES), 1)

        def load_step(i, carry):
            first = pl.multiple_of(i * LANES, LANES)
            for s in range(LANES):
                stage[pl.ds(first + s, 1), :] = mixed[pl.ds(rows_ref[first + s], 1), :]
            return carry

        lax.fori_loop(0, stage.shape[0] // LANES, load_step, 0)

        def inner_step(i, carry):
            batch = pl.ds(pl.multiple_of(i * BATCH, BATCH), BATCH)
            terms = jnp.concatenate(halves(stage[batch, :] * pattern_ref[batch, :].astype(jnp.float32)), axis=1)
            total = jnp.dot(terms, ones_ref[...], preferred_element_type=jnp.float32)
            lines = [jnp.sum(jnp.where(diagonal, total[g * LANES:(g + 1) * LANES], 0.0), axis=0, keepdims=True) for g in range(BATCH // LANES)]
            out_ref[pl.ds(pl.multiple_of(i * (BATCH // LANES), BATCH // LANES), BATCH // LANES), :] = jnp.concatenate(lines, axis=0)
            return carry

        lax.fori_loop(0, stage.shape[0] // BATCH, inner_step, 0)


def local_samples(act, grd, near, far, core, sample_index):
    rows, tokens = act.shape
    width = grd.shape[1]
    count = sample_index.shape[0]
    local = sample_index % (rows * width)
    row, column = local // width, local % width
    where_row = column // LANES * rows + row
    inner = (column % LANES)[:, None] == jnp.arange(LANES, dtype=jnp.int32)[None]
    small = jnp.asarray(sylvester(LANES), jnp.bfloat16)
    pattern = jnp.dot(inner.astype(jnp.bfloat16), small, preferred_element_type=jnp.float32).astype(jnp.bfloat16)
    full = sylvester(rows)
    left, right = full[:, : rows // 2], full[:, rows // 2:]
    tables = np.stack([np.concatenate(pair, axis=1) for pair in ((left, right, left, right), (right, left, right, left))])
    table = lax.dynamic_index_in_dim(jnp.asarray(tables, jnp.bfloat16), core, 0, keepdims=False)
    ones = jnp.ones((2 * LANES, LANES), jnp.bfloat16)
    vmem = pl.BlockSpec(memory_space=pltpu.VMEM)
    out = pl.pallas_call(
        sampled_gradient,
        grid=(width // WIDE,),
        out_shape=jax.ShapeDtypeStruct((count // LANES, LANES), jnp.float32),
        in_specs=[
            pl.BlockSpec(memory_space=pltpu.SMEM),
            vmem,
            pl.BlockSpec((tokens, WIDE), lambda i: (0, i)),
            vmem,
            vmem,
            vmem,
            vmem,
            vmem,
        ],
        out_specs=pl.BlockSpec((count // LANES, LANES), lambda i: (0, 0)),
        scratch_shapes=[
            pltpu.VMEM((rows * width // LANES, LANES), jnp.float32),
            pltpu.VMEM((count, LANES), jnp.float32),
        ],
        compiler_params=pltpu.CompilerParams(vmem_limit_bytes=40 * 1024 * 1024),
        name="sampled_gradient",
    )(where_row, act, grd, near, far, pattern, table, ones)
    return out


def to_all(value, axes):
    size = lax.axis_size(axes)
    return lax.all_to_all(jnp.broadcast_to(value[None], (size,) + value.shape), axes, 0, 0, tiled=True)


def per_device(activations, out_grad, sign_bits, sample_index):
    count, seq_len, columns = activations.shape
    width = out_grad.shape[2]
    chips = lax.axis_size("z")
    here, core = lax.axis_index("z"), lax.axis_index("core")
    swap = [(0, 1), (1, 0)]

    mine = lambda pair: lax.dynamic_index_in_dim(pair, core, 0, keepdims=False)
    other = lambda pair: lax.ppermute(lax.dynamic_index_in_dim(pair, 1 - core, 0, keepdims=False), "core", swap)
    block = jnp.concatenate([mine(out_grad), other(out_grad)], axis=0)
    gathered = lax.all_gather(block, "z", axis=0, tiled=True)
    far = lax.ppermute(sign_bits, "core", swap)
    act = jnp.concatenate([mine(activations), other(activations)], axis=1).T
    act = act.reshape(2 * columns, chips, 2, seq_len // (2 * chips))
    act = jnp.where(core == 0, act, act[:, :, ::-1]).reshape(2 * columns, seq_len)

    terms = local_samples(act, gathered, sign_bits, far, core, sample_index)
    feature_count = sample_index.shape[0]
    per = feature_count // (2 * chips)
    terms = lax.all_to_all(terms.reshape(2 * chips, per), ("z", "core"), 0, 0, tiled=True)
    signs = lax.dynamic_index_in_dim(jnp.asarray(sylvester(chips), jnp.float32), here, 0, keepdims=False)
    scale = 1.0 / (width * float(seq_len) ** 0.5)
    features = jnp.sum(terms.reshape(chips, 2, per) * signs[:, None, None], axis=0) * scale
    everyone = to_all(features, "ex").reshape(-1, per)
    inner = jnp.dot(features, everyone.T, precision=lax.Precision.HIGHEST)
    gram = jnp.sum(to_all(inner, ("z", "core")), axis=0) / feature_count
    return (features, gram)


def solution(mesh):
    params, groups = mesh.devices.shape
    chips = Mesh(mesh.devices.reshape(params // 2, 2, groups), ("z", "core", "ex"))
    param = ("z", "core")
    return jax.shard_map(
        per_device,
        mesh=chips,
        in_specs=(P("ex", None, param), P("ex", param, None), P(param, None), P()),
        out_specs=(P("ex", param), P("ex", None)),
        check_vma=False,
    )
```

```python
import jax
import jax.numpy as jnp
import numpy as np
from jax import lax
from jax.experimental import pallas as pl
from jax.experimental.pallas import tpu as pltpu
from jax.sharding import Mesh, PartitionSpec as P

LANES = 128
WIDE = 2048
BATCH = 1024


def sylvester(order):
    table = np.ones((1, 1), np.float32)
    base = np.array([[1.0, 1.0], [1.0, -1.0]], np.float32)
    while table.shape[0] < order:
        table = np.kron(table, base)
    return table


def halves(value):
    high = value.astype(jnp.bfloat16)
    low = (value - high.astype(jnp.float32)).astype(jnp.bfloat16)
    return high, low


def sampled_gradient(core_ref, rows_ref, act_ref, grd_ref, near_ref, far_ref, pattern_ref, table_ref, ones_ref, out_ref, mixed, stage):
    rows = act_ref.shape[0]
    outer = mixed.shape[0] // rows
    piece = pl.program_id(0)

    value = jnp.dot(act_ref[...], grd_ref[...], preferred_element_type=jnp.float32)
    near, far = value[: rows // 2], value[rows // 2:]
    near = jnp.where(near_ref[...] == 1, near, -near)
    far = jnp.where(far_ref[...] == 1, far, -far)
    parts = [part for half in zip(halves(near), halves(far)) for part in half]
    out = jnp.dot(table_ref[...], jnp.concatenate(parts, axis=0), preferred_element_type=jnp.float32)
    for t in range(WIDE // LANES):
        first = pl.multiple_of((piece * (WIDE // LANES) + t) * rows, rows)
        mixed[pl.ds(first, rows), :] = out[:, t * LANES:(t + 1) * LANES]

    @pl.when(piece == pl.num_programs(0) - 1)
    def _():
        def outer_step(i, carry):
            first = pl.multiple_of(i * 8, 8)
            tiles = [mixed[pl.ds(pl.multiple_of(m * rows + first, 8), 8), :] for m in range(outer)]
            step = 1
            while step < outer:
                tiles = [tiles[m ^ step] - tiles[m] if m & step else tiles[m] + tiles[m ^ step] for m in range(outer)]
                step *= 2
            for m in range(outer):
                mixed[pl.ds(pl.multiple_of(m * rows + first, 8), 8), :] = tiles[m]
            return carry

        lax.fori_loop(0, rows // 8, outer_step, 0)

        diagonal = lax.broadcasted_iota(jnp.int32, (LANES, LANES), 0) == lax.broadcasted_iota(jnp.int32, (LANES, LANES), 1)

        def load_step(i, carry):
            first = pl.multiple_of(i * LANES, LANES)
            for s in range(LANES):
                stage[pl.ds(first + s, 1), :] = mixed[pl.ds(rows_ref[first + s], 1), :]
            return carry

        lax.fori_loop(0, stage.shape[0] // LANES, load_step, 0)

        def inner_step(i, carry):
            batch = pl.ds(pl.multiple_of(i * BATCH, BATCH), BATCH)
            terms = jnp.concatenate(halves(stage[batch, :] * pattern_ref[batch, :].astype(jnp.float32)), axis=1)
            total = jnp.dot(terms, ones_ref[...], preferred_element_type=jnp.float32)
            lines = [jnp.sum(jnp.where(diagonal, total[g * LANES:(g + 1) * LANES], 0.0), axis=0, keepdims=True) for g in range(BATCH // LANES)]
            out_ref[pl.ds(pl.multiple_of(i * (BATCH // LANES), BATCH // LANES), BATCH // LANES), :] = jnp.concatenate(lines, axis=0)
            return carry

        lax.fori_loop(0, stage.shape[0] // BATCH, inner_step, 0)


def local_samples(act, grd, near, far, core, sample_index):
    rows, tokens = act.shape
    width = grd.shape[2]
    count = sample_index.shape[0]
    local = sample_index % (rows * width)
    row, column = local // width, local % width
    where_row = column // LANES * rows + row
    inner = (column % LANES)[:, None] == jnp.arange(LANES, dtype=jnp.int32)[None]
    small = jnp.asarray(sylvester(LANES), jnp.bfloat16)
    pattern = jnp.dot(inner.astype(jnp.bfloat16), small, preferred_element_type=jnp.float32).astype(jnp.bfloat16)
    full = sylvester(rows)
    left, right = full[:, : rows // 2], full[:, rows // 2:]
    tables = np.stack([np.concatenate(pair, axis=1) for pair in ((left, right, left, right), (right, left, right, left))])
    table = lax.dynamic_index_in_dim(jnp.asarray(tables, jnp.bfloat16), core, 0, keepdims=False)
    ones = jnp.ones((2 * LANES, LANES), jnp.bfloat16)
    vmem = pl.BlockSpec(memory_space=pltpu.VMEM)
    out = pl.pallas_call(
        sampled_gradient,
        grid_spec=pltpu.PrefetchScalarGridSpec(
            num_scalar_prefetch=2,
            grid=(width // WIDE,),
            in_specs=[
                vmem,
                pl.BlockSpec((None, tokens, WIDE), lambda i, which, _: (which[0], 0, i)),
                pl.BlockSpec((rows // 2, WIDE), lambda i, *_: (0, i)),
                pl.BlockSpec((rows // 2, WIDE), lambda i, *_: (0, i)),
                vmem,
                vmem,
                vmem,
            ],
            out_specs=pl.BlockSpec((count // LANES, LANES), lambda i, *_: (0, 0)),
            scratch_shapes=[
                pltpu.VMEM((rows * width // LANES, LANES), jnp.float32),
                pltpu.VMEM((count, LANES), jnp.float32),
            ],
        ),
        out_shape=jax.ShapeDtypeStruct((count // LANES, LANES), jnp.float32),
        compiler_params=pltpu.CompilerParams(vmem_limit_bytes=40 * 1024 * 1024),
        name="sampled_gradient",
    )(core[None], where_row, act, grd, near, far, pattern, table, ones)
    return out


def to_all(value, axes):
    size = lax.axis_size(axes)
    return lax.all_to_all(jnp.broadcast_to(value[None], (size,) + value.shape), axes, 0, 0, tiled=True)


def per_device(activations, out_grad, sign_bits, sample_index):
    count, seq_len, columns = activations.shape
    width = out_grad.shape[2]
    chips = lax.axis_size("z")
    here, core = lax.axis_index("z"), lax.axis_index("core")
    swap = [(0, 1), (1, 0)]

    mine = lambda pair: lax.dynamic_index_in_dim(pair, core, 0, keepdims=False)
    other = lambda pair: lax.ppermute(lax.dynamic_index_in_dim(pair, 1 - core, 0, keepdims=False), "core", swap)
    gathered = lax.all_gather(out_grad, ("z", "core"), axis=1, tiled=True)
    far = lax.ppermute(sign_bits, "core", swap)
    act = jnp.concatenate([mine(activations), other(activations)], axis=1).T

    terms = local_samples(act, gathered, sign_bits, far, core, sample_index)
    feature_count = sample_index.shape[0]
    per = feature_count // (2 * chips)
    terms = lax.all_to_all(terms.reshape(2 * chips, per), ("z", "core"), 0, 0, tiled=True)
    signs = lax.dynamic_index_in_dim(jnp.asarray(sylvester(chips), jnp.float32), here, 0, keepdims=False)
    scale = 1.0 / (width * float(seq_len) ** 0.5)
    features = jnp.sum(terms.reshape(chips, 2, per) * signs[:, None, None], axis=0) * scale
    everyone = to_all(features, "ex").reshape(-1, per)
    inner = jnp.dot(features, everyone.T, precision=lax.Precision.HIGHEST)
    gram = jnp.sum(to_all(inner, ("z", "core")), axis=0) / feature_count
    return (features, gram)


def solution(mesh):
    params, groups = mesh.devices.shape
    chips = Mesh(mesh.devices.reshape(params // 2, 2, groups), ("z", "core", "ex"))
    param = ("z", "core")
    return jax.shard_map(
        per_device,
        mesh=chips,
        in_specs=(P("ex", None, param), P("ex", param, None), P(param, None), P()),
        out_specs=(P("ex", param), P("ex", None)),
        check_vma=False,
    )
```

```python
import jax
import jax.numpy as jnp
import numpy as np
from jax import lax
from jax.experimental import pallas as pl
from jax.experimental.pallas import tpu as pltpu
from jax.sharding import Mesh, PartitionSpec as P

LANES = 128
WIDE = 2048
BATCH = 1024
LOAD = 512
VMEM_MIB = 60


def sylvester(order):
    table = np.ones((1, 1), np.float32)
    base = np.array([[1.0, 1.0], [1.0, -1.0]], np.float32)
    while table.shape[0] < order:
        table = np.kron(table, base)
    return table


def halves(value):
    high = value.astype(jnp.bfloat16)
    low = (value - high.astype(jnp.float32)).astype(jnp.bfloat16)
    return high, low


def sampled_gradient(place_ref, index_ref, near_act_ref, far_act_ref, far_ref, table_ref, small_ref, near_ref, *refs):
    grd_refs, (out_ref, mixed, stage, signs, tokens, act, rows_v, rows_s, sem) = refs[:-9], refs[-9:]
    rows = act.shape[0]
    outer = mixed.shape[0] // rows
    width = outer * LANES
    piece, last = pl.program_id(0), pl.num_programs(0) - 1
    core = place_ref[0]
    row_copy = pltpu.make_async_copy(rows_v, rows_s, sem)

    @pl.when(piece == 0)
    def _():
        index = index_ref[...]
        row = (index // width) % rows
        rows_v[...] = (index % width) // LANES * rows + row
        row_copy.start()
        chips = len(grd_refs) // 2
        depth = grd_refs[0].shape[0]
        for which in range(2):
            for j in range(chips):
                source = lax.rem(place_ref[1] + j, chips) * (2 * depth) + lax.rem(core + which, 2) * depth
                source = pl.ds(pl.multiple_of(source, depth), depth)
                target = pl.ds((which * chips + j) * depth, depth)
                tokens[target, :rows // 2] = near_act_ref[core, source, :]
                tokens[target, rows // 2:] = far_act_ref[core, source, :]
        act[...] = tokens[...].T

    grd = jnp.concatenate([ref[...] for ref in grd_refs], axis=0)
    value = jnp.dot(act[...], grd, preferred_element_type=jnp.float32)
    near, far = value[: rows // 2], value[rows // 2:]
    columns = pl.ds(pl.multiple_of(piece * WIDE, WIDE), WIDE)
    near = jnp.where(near_ref[...] == 1, near, -near)
    far = jnp.where(far_ref[:, columns] == 1, far, -far)
    parts = [part for half in zip(halves(near), halves(far)) for part in half]
    out = jnp.dot(table_ref[core], jnp.concatenate(parts, axis=0), preferred_element_type=jnp.float32)
    for t in range(WIDE // LANES):
        first = pl.multiple_of((piece * (WIDE // LANES) + t) * rows, rows)
        mixed[pl.ds(first, rows), :] = out[:, t * LANES:(t + 1) * LANES]

    @pl.when(piece == last)
    def _():
        def outer_step(i, carry):
            first = pl.multiple_of(i * 8, 8)
            tiles = [mixed[pl.ds(pl.multiple_of(m * rows + first, 8), 8), :] for m in range(outer)]
            step = 1
            while step < outer:
                tiles = [tiles[m ^ step] - tiles[m] if m & step else tiles[m] + tiles[m ^ step] for m in range(outer)]
                step *= 2
            for m in range(outer):
                mixed[pl.ds(pl.multiple_of(m * rows + first, 8), 8), :] = tiles[m]
            return carry

        lax.fori_loop(0, rows // 8, outer_step, 0)

        row_copy.wait()

        across = lax.broadcasted_iota(jnp.int32, (LANES, LANES), 1)
        diagonal = lax.broadcasted_iota(jnp.int32, (LANES, LANES), 0) == across
        ones = jnp.ones((2 * LANES, LANES), jnp.bfloat16)

        def load_step(i, carry):
            first = pl.multiple_of(i * LOAD, LOAD)
            group = pl.ds(pl.multiple_of(i * (LOAD // LANES), LOAD // LANES), LOAD // LANES)
            inner = (index_ref[group, :] % LANES).astype(jnp.float32)
            spread = [jnp.where(diagonal, inner[g:g + 1, :], 0.0).astype(jnp.bfloat16) for g in range(LOAD // LANES)]
            spread = jnp.dot(jnp.concatenate(spread, axis=0), ones[:LANES], preferred_element_type=jnp.float32)
            lane = lax.broadcasted_iota(jnp.int32, (LOAD, LANES), 1).astype(jnp.float32)
            chosen = jnp.where(spread == lane, 1.0, 0.0).astype(jnp.bfloat16)
            pattern = jnp.dot(chosen, small_ref[...], preferred_element_type=jnp.float32)
            signs[pl.ds(first, LOAD), :] = pattern.astype(jnp.bfloat16)
            for s in range(LOAD):
                stage[pl.ds(first + s, 1), :] = mixed[pl.ds(rows_s[i * (LOAD // LANES) + s // LANES, s % LANES], 1), :]
            return carry

        lax.fori_loop(0, stage.shape[0] // LOAD, load_step, 0)

        def inner_step(i, carry):
            batch = pl.ds(pl.multiple_of(i * BATCH, BATCH), BATCH)
            terms = jnp.concatenate(halves(stage[batch, :] * signs[batch, :].astype(jnp.float32)), axis=1)
            total = jnp.dot(terms, ones, preferred_element_type=jnp.float32)
            lines = BATCH // LANES
            sums = [jnp.sum(jnp.where(diagonal, total[g * LANES:(g + 1) * LANES], 0.0), axis=0, keepdims=True) for g in range(lines)]
            out_ref[pl.ds(pl.multiple_of(i * lines, lines), lines), :] = jnp.concatenate(sums, axis=0)
            return carry

        lax.fori_loop(0, stage.shape[0] // BATCH, inner_step, 0)


def local_samples(near_act, far_act, blocks, near, far, core, here, sample_index):
    tokens = near_act.shape[1]
    rows = 2 * near_act.shape[2]
    width = near.shape[1]
    count = sample_index.shape[0]
    full = sylvester(rows)
    left, right = full[:, : rows // 2], full[:, rows // 2:]
    tables = np.stack([np.concatenate(pair, axis=1) for pair in ((left, right, left, right), (right, left, right, left))])
    vmem = pl.BlockSpec(memory_space=pltpu.VMEM)
    return pl.pallas_call(
        sampled_gradient,
        grid=(width // WIDE,),
        out_shape=jax.ShapeDtypeStruct((count // LANES, LANES), jnp.float32),
        in_specs=[pl.BlockSpec(memory_space=pltpu.SMEM)]
        + [vmem] * 6
        + [pl.BlockSpec((part.shape[0], WIDE), lambda i: (0, i)) for part in (near, *blocks)],
        out_specs=pl.BlockSpec((count // LANES, LANES), lambda i: (0, 0)),
        scratch_shapes=[
            pltpu.VMEM((rows * width // LANES, LANES), jnp.float32),
            pltpu.VMEM((count, LANES), jnp.float32),
            pltpu.VMEM((count, LANES), jnp.bfloat16),
            pltpu.VMEM((tokens, rows), jnp.bfloat16),
            pltpu.VMEM((rows, tokens), jnp.bfloat16),
            pltpu.VMEM((count // LANES, LANES), jnp.int32),
            pltpu.SMEM((count // LANES, LANES), jnp.int32),
            pltpu.SemaphoreType.DMA,
        ],
        compiler_params=pltpu.CompilerParams(vmem_limit_bytes=VMEM_MIB * 1024 * 1024),
        name="sampled_gradient",
    )(
        jnp.stack([core, here]).astype(jnp.int32),
        sample_index.reshape(count // LANES, LANES),
        near_act,
        far_act,
        far,
        jnp.asarray(tables, jnp.bfloat16),
        jnp.asarray(sylvester(LANES), jnp.bfloat16),
        near,
        *blocks,
    )


def around(blocks, axis):
    size = lax.axis_size(axis)
    up = [(i, (i + 1) % size) for i in range(size)]
    down = [(i, (i - 1) % size) for i in range(size)]
    ups, downs = [[[block] for block in blocks] for _ in range(2)]
    for step in range(size // 2):
        for chain in ups:
            chain.append(lax.ppermute(chain[-1], axis, up))
        if step < (size - 1) // 2:
            for chain in downs:
                chain.append(lax.ppermute(chain[-1], axis, down))
    return [part for one, two in zip(downs, ups) for part in one + two[:0:-1]]


def to_all(value, axes):
    size = lax.axis_size(axes)
    return lax.all_to_all(jnp.broadcast_to(value[None], (size,) + value.shape), axes, 0, 0, tiled=True)


def per_device(activations, out_grad, sign_bits, sample_index):
    seq_len, width = activations.shape[1], out_grad.shape[2]
    chips = lax.axis_size("z")
    here, core = lax.axis_index("z"), lax.axis_index("core")
    swap = [(0, 1), (1, 0)]

    mine = lax.dynamic_index_in_dim(out_grad, core, 0, keepdims=False)
    other = lax.ppermute(lax.dynamic_index_in_dim(out_grad, 1 - core, 0, keepdims=False), "core", swap)
    far_act = lax.ppermute(activations, "core", swap)
    far = lax.ppermute(sign_bits, "core", swap)
    blocks = around([mine, other], "z")

    terms = local_samples(activations, far_act, blocks, sign_bits, far, core, here, sample_index)
    feature_count = sample_index.shape[0]
    per = feature_count // (2 * chips)
    terms = lax.all_to_all(terms.reshape(2 * chips, per), ("z", "core"), 0, 0, tiled=True)
    signs = lax.dynamic_index_in_dim(jnp.asarray(sylvester(chips), jnp.float32), here, 0, keepdims=False)
    scale = 1.0 / (width * float(seq_len) ** 0.5)
    features = jnp.sum(terms.reshape(chips, 2, per) * signs[:, None, None], axis=0) * scale
    everyone = to_all(features, "ex").reshape(-1, per)
    inner = jnp.dot(features, everyone.T, precision=lax.Precision.HIGHEST)
    gram = jnp.sum(to_all(inner, ("z", "core")), axis=0) / feature_count
    return (features, gram)


def solution(mesh):
    params, groups = mesh.devices.shape
    chips = Mesh(mesh.devices.reshape(params // 2, 2, groups), ("z", "core", "ex"))
    param = ("z", "core")
    return jax.shard_map(
        per_device,
        mesh=chips,
        in_specs=(P("ex", None, param), P("ex", param, None), P(param, None), P()),
        out_specs=(P("ex", param), P("ex", None)),
        check_vma=False,
    )
```

```python
import jax
import jax.numpy as jnp
import numpy as np
from jax import lax
from jax.experimental import pallas as pl
from jax.experimental.pallas import tpu as pltpu
from jax.sharding import Mesh, PartitionSpec as P

LANES = 128
WIDE = 2048
BATCH = 4096
LOAD = 512
VMEM_MIB = 60


def sylvester(order):
    table = np.ones((1, 1), np.float32)
    base = np.array([[1.0, 1.0], [1.0, -1.0]], np.float32)
    while table.shape[0] < order:
        table = np.kron(table, base)
    return table


def halves(value):
    high = value.astype(jnp.bfloat16)
    low = (value - high.astype(jnp.float32)).astype(jnp.bfloat16)
    return high, low


def sampled_gradient(place_ref, index_ref, near_act_ref, far_act_ref, far_ref, table_ref, small_ref, near_ref, *refs):
    grd_refs, (out_ref, mixed, stage, signs, tokens, act, rows_v, rows_s, sem) = refs[:-9], refs[-9:]
    rows = act.shape[0]
    outer = mixed.shape[0] // rows
    width = outer * LANES
    piece, last = pl.program_id(0), pl.num_programs(0) - 1
    core = place_ref[0]
    row_copy = pltpu.make_async_copy(rows_v, rows_s, sem)

    @pl.when(piece == 0)
    def _():
        index = index_ref[...]
        row = (index // width) % rows
        rows_v[...] = (index % width) // LANES * rows + row
        row_copy.start()
        chips = len(grd_refs) // 2
        depth = grd_refs[0].shape[0]
        for which in range(2):
            for j in range(chips):
                source = lax.rem(place_ref[1] + j, chips) * (2 * depth) + lax.rem(core + which, 2) * depth
                source = pl.ds(pl.multiple_of(source, depth), depth)
                target = pl.ds((which * chips + j) * depth, depth)
                tokens[target, :rows // 2] = near_act_ref[core, source, :]
                tokens[target, rows // 2:] = far_act_ref[core, source, :]
        act[...] = tokens[...].T

    grd = jnp.concatenate([ref[...] for ref in grd_refs], axis=0)
    value = jnp.dot(act[...], grd, preferred_element_type=jnp.float32)
    near, far = value[: rows // 2], value[rows // 2:]
    columns = pl.ds(pl.multiple_of(piece * WIDE, WIDE), WIDE)
    near = jnp.where(near_ref[...] == 1, near, -near)
    far = jnp.where(far_ref[:, columns] == 1, far, -far)
    parts = [part for half in zip(halves(near), halves(far)) for part in half]
    out = jnp.dot(table_ref[core], jnp.concatenate(parts, axis=0), preferred_element_type=jnp.float32)
    for t in range(WIDE // LANES):
        first = pl.multiple_of((piece * (WIDE // LANES) + t) * rows, rows)
        mixed[pl.ds(first, rows), :] = out[:, t * LANES:(t + 1) * LANES]

    @pl.when(piece == last)
    def _():
        def outer_step(i, carry):
            first = pl.multiple_of(i * 8, 8)
            tiles = [mixed[pl.ds(pl.multiple_of(m * rows + first, 8), 8), :] for m in range(outer)]
            step = 1
            while step < outer:
                tiles = [tiles[m ^ step] - tiles[m] if m & step else tiles[m] + tiles[m ^ step] for m in range(outer)]
                step *= 2
            for m in range(outer):
                mixed[pl.ds(pl.multiple_of(m * rows + first, 8), 8), :] = tiles[m]
            return carry

        lax.fori_loop(0, rows // 8, outer_step, 0)

        row_copy.wait()

        across = lax.broadcasted_iota(jnp.int32, (LANES, LANES), 1)
        diagonal = lax.broadcasted_iota(jnp.int32, (LANES, LANES), 0) == across
        ones = jnp.ones((2 * LANES, LANES), jnp.bfloat16)

        def load_step(i, carry):
            first = pl.multiple_of(i * LOAD, LOAD)
            group = pl.ds(pl.multiple_of(i * (LOAD // LANES), LOAD // LANES), LOAD // LANES)
            inner = (index_ref[group, :] % LANES).astype(jnp.float32)
            spread = [jnp.where(diagonal, inner[g:g + 1, :], 0.0).astype(jnp.bfloat16) for g in range(LOAD // LANES)]
            spread = jnp.dot(jnp.concatenate(spread, axis=0), ones[:LANES], preferred_element_type=jnp.float32)
            lane = lax.broadcasted_iota(jnp.int32, (LOAD, LANES), 1).astype(jnp.float32)
            chosen = jnp.where(spread == lane, 1.0, 0.0).astype(jnp.bfloat16)
            pattern = jnp.dot(chosen, small_ref[...], preferred_element_type=jnp.float32)
            signs[pl.ds(first, LOAD), :] = pattern.astype(jnp.bfloat16)
            for s in range(LOAD):
                stage[pl.ds(first + s, 1), :] = mixed[pl.ds(rows_s[i * (LOAD // LANES) + s // LANES, s % LANES], 1), :]
            return carry

        lax.fori_loop(0, stage.shape[0] // LOAD, load_step, 0)

        def inner_step(i, carry):
            batch = pl.ds(pl.multiple_of(i * BATCH, BATCH), BATCH)
            terms = jnp.concatenate(halves(stage[batch, :] * signs[batch, :].astype(jnp.float32)), axis=1)
            total = jnp.dot(terms, ones, preferred_element_type=jnp.float32)
            lines = BATCH // LANES
            sums = [jnp.sum(jnp.where(diagonal, total[g * LANES:(g + 1) * LANES], 0.0), axis=0, keepdims=True) for g in range(lines)]
            out_ref[pl.ds(pl.multiple_of(i * lines, lines), lines), :] = jnp.concatenate(sums, axis=0)
            return carry

        lax.fori_loop(0, stage.shape[0] // BATCH, inner_step, 0)


def local_samples(near_act, far_act, blocks, near, far, core, here, sample_index):
    tokens = near_act.shape[1]
    rows = 2 * near_act.shape[2]
    width = near.shape[1]
    count = sample_index.shape[0]
    full = sylvester(rows)
    left, right = full[:, : rows // 2], full[:, rows // 2:]
    tables = np.stack([np.concatenate(pair, axis=1) for pair in ((left, right, left, right), (right, left, right, left))])
    vmem = pl.BlockSpec(memory_space=pltpu.VMEM)
    return pl.pallas_call(
        sampled_gradient,
        grid=(width // WIDE,),
        out_shape=jax.ShapeDtypeStruct((count // LANES, LANES), jnp.float32),
        in_specs=[pl.BlockSpec(memory_space=pltpu.SMEM)]
        + [vmem] * 6
        + [pl.BlockSpec((part.shape[0], WIDE), lambda i: (0, i)) for part in (near, *blocks)],
        out_specs=pl.BlockSpec((count // LANES, LANES), lambda i: (0, 0)),
        scratch_shapes=[
            pltpu.VMEM((rows * width // LANES, LANES), jnp.float32),
            pltpu.VMEM((count, LANES), jnp.float32),
            pltpu.VMEM((count, LANES), jnp.bfloat16),
            pltpu.VMEM((tokens, rows), jnp.bfloat16),
            pltpu.VMEM((rows, tokens), jnp.bfloat16),
            pltpu.VMEM((count // LANES, LANES), jnp.int32),
            pltpu.SMEM((count // LANES, LANES), jnp.int32),
            pltpu.SemaphoreType.DMA,
        ],
        compiler_params=pltpu.CompilerParams(vmem_limit_bytes=VMEM_MIB * 1024 * 1024),
        name="sampled_gradient",
    )(
        jnp.stack([core, here]).astype(jnp.int32),
        sample_index.reshape(count // LANES, LANES),
        near_act,
        far_act,
        far,
        jnp.asarray(tables, jnp.bfloat16),
        jnp.asarray(sylvester(LANES), jnp.bfloat16),
        near,
        *blocks,
    )


def around(blocks, axis):
    size = lax.axis_size(axis)
    up = [(i, (i + 1) % size) for i in range(size)]
    down = [(i, (i - 1) % size) for i in range(size)]
    ups, downs = [[[block] for block in blocks] for _ in range(2)]
    for _ in range(size // 2 - 1):
        for chain in ups:
            chain.append(lax.ppermute(chain[-1], axis, up))
        for chain in downs:
            chain.append(lax.ppermute(chain[-1], axis, down))
    ups[0].append(lax.ppermute(ups[0][-1], axis, up))
    downs[1].append(lax.ppermute(downs[1][-1], axis, down))
    return [part for one, two in zip(downs, ups) for part in one + two[:0:-1]]


def to_all(value, axes):
    size = lax.axis_size(axes)
    return lax.all_to_all(jnp.broadcast_to(value[None], (size,) + value.shape), axes, 0, 0, tiled=True)


def per_device(activations, out_grad, sign_bits, sample_index):
    seq_len, width = activations.shape[1], out_grad.shape[2]
    chips = lax.axis_size("z")
    here, core = lax.axis_index("z"), lax.axis_index("core")
    swap = [(0, 1), (1, 0)]

    mine = lax.dynamic_index_in_dim(out_grad, core, 0, keepdims=False)
    other = lax.ppermute(lax.dynamic_index_in_dim(out_grad, 1 - core, 0, keepdims=False), "core", swap)
    far_act = lax.ppermute(activations, "core", swap)
    far = lax.ppermute(sign_bits, "core", swap)
    blocks = around([mine, other], "z")

    terms = local_samples(activations, far_act, blocks, sign_bits, far, core, here, sample_index)
    feature_count = sample_index.shape[0]
    per = feature_count // (2 * chips)
    terms = lax.all_to_all(terms.reshape(2 * chips, per), ("z", "core"), 0, 0, tiled=True)
    signs = lax.dynamic_index_in_dim(jnp.asarray(sylvester(chips), jnp.float32), here, 0, keepdims=False)
    scale = 1.0 / (width * float(seq_len) ** 0.5)
    features = jnp.sum(terms.reshape(chips, 2, per) * signs[:, None, None], axis=0) * scale
    everyone = to_all(features, "ex").reshape(-1, per)
    inner = jnp.dot(features, everyone.T, precision=lax.Precision.HIGHEST)
    gram = jnp.sum(to_all(inner, ("z", "core")), axis=0) / feature_count
    return (features, gram)


def solution(mesh):
    params, groups = mesh.devices.shape
    chips = Mesh(mesh.devices.reshape(params // 2, 2, groups), ("z", "core", "ex"))
    param = ("z", "core")
    return jax.shard_map(
        per_device,
        mesh=chips,
        in_specs=(P("ex", None, param), P("ex", param, None), P(param, None), P()),
        out_specs=(P("ex", param), P("ex", None)),
        check_vma=False,
    )
```

```python
import jax
import jax.numpy as jnp
import numpy as np
from jax import lax
from jax.experimental import pallas as pl
from jax.experimental.pallas import tpu as pltpu
from jax.sharding import Mesh, PartitionSpec as P

LANES = 128
WIDE = 2048
BATCH = 4096
LOAD = 512
VMEM_MIB = 60


def sylvester(order):
    table = np.ones((1, 1), np.float32)
    base = np.array([[1.0, 1.0], [1.0, -1.0]], np.float32)
    while table.shape[0] < order:
        table = np.kron(table, base)
    return table


def halves(value):
    high = value.astype(jnp.bfloat16)
    low = (value - high.astype(jnp.float32)).astype(jnp.bfloat16)
    return high, low


def sampled_gradient(place_ref, index_ref, near_act_ref, far_act_ref, far_ref, table_ref, small_ref, near_ref, *refs):
    grd_refs, (out_ref, mixed, stage, signs, tokens, act, rows_v, rows_s, sem) = refs[:-9], refs[-9:]
    rows = act.shape[0]
    outer = mixed.shape[0] // rows
    width = outer * LANES
    piece, last = pl.program_id(0), pl.num_programs(0) - 1
    core = place_ref[0]
    row_copy = pltpu.make_async_copy(rows_v, rows_s, sem)

    @pl.when(piece == 0)
    def _():
        index = index_ref[...]
        row = (index // width) % rows
        rows_v[...] = (index % width) // LANES * rows + row
        row_copy.start()
        chips = len(grd_refs) // 2
        depth = grd_refs[0].shape[0]
        for which in range(2):
            for j in range(chips):
                source = lax.rem(place_ref[1] + j, chips) * (2 * depth) + lax.rem(core + which, 2) * depth
                source = pl.ds(pl.multiple_of(source, depth), depth)
                target = pl.ds((which * chips + j) * depth, depth)
                tokens[target, :rows // 2] = near_act_ref[core, source, :]
                tokens[target, rows // 2:] = far_act_ref[core, source, :]
        act[...] = tokens[...].T

    grd = jnp.concatenate([ref[...] for ref in grd_refs], axis=0)
    value = jnp.dot(act[...], grd, preferred_element_type=jnp.float32)
    near, far = value[: rows // 2], value[rows // 2:]
    columns = pl.ds(pl.multiple_of(piece * WIDE, WIDE), WIDE)
    near = near * near_ref[...].astype(jnp.float32)
    far = far * far_ref[:, columns].astype(jnp.float32)
    parts = [part for half in zip(halves(near), halves(far)) for part in half]
    out = jnp.dot(table_ref[core], jnp.concatenate(parts, axis=0), preferred_element_type=jnp.float32)
    for t in range(WIDE // LANES):
        first = pl.multiple_of((piece * (WIDE // LANES) + t) * rows, rows)
        mixed[pl.ds(first, rows), :] = out[:, t * LANES:(t + 1) * LANES]

    @pl.when(piece == last)
    def _():
        def outer_step(i, carry):
            first = pl.multiple_of(i * 8, 8)
            tiles = [mixed[pl.ds(pl.multiple_of(m * rows + first, 8), 8), :] for m in range(outer)]
            step = 1
            while step < outer:
                tiles = [tiles[m ^ step] - tiles[m] if m & step else tiles[m] + tiles[m ^ step] for m in range(outer)]
                step *= 2
            for m in range(outer):
                mixed[pl.ds(pl.multiple_of(m * rows + first, 8), 8), :] = tiles[m]
            return carry

        lax.fori_loop(0, rows // 8, outer_step, 0)

        row_copy.wait()

        across = lax.broadcasted_iota(jnp.int32, (LANES, LANES), 1)
        diagonal = lax.broadcasted_iota(jnp.int32, (LANES, LANES), 0) == across
        ones = jnp.ones((2 * LANES, LANES), jnp.bfloat16)

        def load_step(i, carry):
            first = pl.multiple_of(i * LOAD, LOAD)
            group = pl.ds(pl.multiple_of(i * (LOAD // LANES), LOAD // LANES), LOAD // LANES)
            inner = (index_ref[group, :] % LANES).astype(jnp.float32)
            spread = [jnp.where(diagonal, inner[g:g + 1, :], 0.0).astype(jnp.bfloat16) for g in range(LOAD // LANES)]
            spread = jnp.dot(jnp.concatenate(spread, axis=0), ones[:LANES], preferred_element_type=jnp.float32)
            lane = lax.broadcasted_iota(jnp.int32, (LOAD, LANES), 1).astype(jnp.float32)
            chosen = jnp.where(spread == lane, 1.0, 0.0).astype(jnp.bfloat16)
            pattern = jnp.dot(chosen, small_ref[...], preferred_element_type=jnp.float32)
            signs[pl.ds(first, LOAD), :] = pattern.astype(jnp.bfloat16)
            for s in range(LOAD):
                stage[pl.ds(first + s, 1), :] = mixed[pl.ds(rows_s[i * (LOAD // LANES) + s // LANES, s % LANES], 1), :]
            return carry

        lax.fori_loop(0, stage.shape[0] // LOAD, load_step, 0)

        def inner_step(i, carry):
            batch = pl.ds(pl.multiple_of(i * BATCH, BATCH), BATCH)
            terms = jnp.concatenate(halves(stage[batch, :] * signs[batch, :].astype(jnp.float32)), axis=1)
            total = jnp.dot(terms, ones, preferred_element_type=jnp.float32)
            lines = BATCH // LANES
            sums = [jnp.sum(jnp.where(diagonal, total[g * LANES:(g + 1) * LANES], 0.0), axis=0, keepdims=True) for g in range(lines)]
            out_ref[pl.ds(pl.multiple_of(i * lines, lines), lines), :] = jnp.concatenate(sums, axis=0)
            return carry

        lax.fori_loop(0, stage.shape[0] // BATCH, inner_step, 0)


def local_samples(near_act, far_act, blocks, near, far, core, here, sample_index):
    tokens = near_act.shape[1]
    rows = 2 * near_act.shape[2]
    width = near.shape[1]
    count = sample_index.shape[0]
    full = sylvester(rows)
    left, right = full[:, : rows // 2], full[:, rows // 2:]
    tables = np.stack([np.concatenate(pair, axis=1) for pair in ((left, right, left, right), (right, left, right, left))])
    vmem = pl.BlockSpec(memory_space=pltpu.VMEM)
    return pl.pallas_call(
        sampled_gradient,
        grid=(width // WIDE,),
        out_shape=jax.ShapeDtypeStruct((count // LANES, LANES), jnp.float32),
        in_specs=[pl.BlockSpec(memory_space=pltpu.SMEM)]
        + [vmem] * 6
        + [pl.BlockSpec((part.shape[0], WIDE), lambda i: (0, i)) for part in (near, *blocks)],
        out_specs=pl.BlockSpec((count // LANES, LANES), lambda i: (0, 0)),
        scratch_shapes=[
            pltpu.VMEM((rows * width // LANES, LANES), jnp.float32),
            pltpu.VMEM((count, LANES), jnp.float32),
            pltpu.VMEM((count, LANES), jnp.bfloat16),
            pltpu.VMEM((tokens, rows), jnp.bfloat16),
            pltpu.VMEM((rows, tokens), jnp.bfloat16),
            pltpu.VMEM((count // LANES, LANES), jnp.int32),
            pltpu.SMEM((count // LANES, LANES), jnp.int32),
            pltpu.SemaphoreType.DMA,
        ],
        compiler_params=pltpu.CompilerParams(vmem_limit_bytes=VMEM_MIB * 1024 * 1024),
        name="sampled_gradient",
    )(
        jnp.stack([core, here]).astype(jnp.int32),
        sample_index.reshape(count // LANES, LANES),
        near_act,
        far_act,
        far,
        jnp.asarray(tables, jnp.bfloat16),
        jnp.asarray(sylvester(LANES), jnp.bfloat16),
        near,
        *blocks,
    )


def around(blocks, axis):
    size = lax.axis_size(axis)
    up = [(i, (i + 1) % size) for i in range(size)]
    down = [(i, (i - 1) % size) for i in range(size)]
    ups, downs = [[[block] for block in blocks] for _ in range(2)]
    for _ in range(size // 2 - 1):
        for chain in ups:
            chain.append(lax.ppermute(chain[-1], axis, up))
        for chain in downs:
            chain.append(lax.ppermute(chain[-1], axis, down))
    ups[0].append(lax.ppermute(ups[0][-1], axis, up))
    downs[1].append(lax.ppermute(downs[1][-1], axis, down))
    return [part for one, two in zip(downs, ups) for part in one + two[:0:-1]]


def to_all(value, axes):
    size = lax.axis_size(axes)
    return lax.all_to_all(jnp.broadcast_to(value[None], (size,) + value.shape), axes, 0, 0, tiled=True)


def per_device(activations, out_grad, sign_bits, sample_index):
    seq_len, width = activations.shape[1], out_grad.shape[2]
    chips = lax.axis_size("z")
    here, core = lax.axis_index("z"), lax.axis_index("core")
    swap = [(0, 1), (1, 0)]

    mine = lax.dynamic_index_in_dim(out_grad, core, 0, keepdims=False)
    other = lax.ppermute(lax.dynamic_index_in_dim(out_grad, 1 - core, 0, keepdims=False), "core", swap)
    far_act = lax.ppermute(activations, "core", swap)
    near = jnp.where(sign_bits == 1, 1.0, -1.0).astype(jnp.bfloat16)
    far = lax.ppermute(near, "core", swap)
    blocks = around([mine, other], "z")

    terms = local_samples(activations, far_act, blocks, near, far, core, here, sample_index)
    feature_count = sample_index.shape[0]
    per = feature_count // (2 * chips)
    terms = lax.all_to_all(terms.reshape(2 * chips, per), ("z", "core"), 0, 0, tiled=True)
    signs = lax.dynamic_index_in_dim(jnp.asarray(sylvester(chips), jnp.float32), here, 0, keepdims=False)
    scale = 1.0 / (width * float(seq_len) ** 0.5)
    features = jnp.sum(terms.reshape(chips, 2, per) * signs[:, None, None], axis=0) * scale
    everyone = to_all(features, "ex").reshape(-1, per)
    inner = jnp.dot(features, everyone.T, precision=lax.Precision.HIGHEST)
    gram = jnp.sum(to_all(inner, ("z", "core")), axis=0) / feature_count
    return (features, gram)


def solution(mesh):
    params, groups = mesh.devices.shape
    chips = Mesh(mesh.devices.reshape(params // 2, 2, groups), ("z", "core", "ex"))
    param = ("z", "core")
    return jax.shard_map(
        per_device,
        mesh=chips,
        in_specs=(P("ex", None, param), P("ex", param, None), P(param, None), P()),
        out_specs=(P("ex", param), P("ex", None)),
        check_vma=False,
    )
```

```python
import jax
import jax.numpy as jnp
import numpy as np
from jax import lax
from jax.experimental import pallas as pl
from jax.experimental.pallas import tpu as pltpu
from jax.sharding import Mesh, PartitionSpec as P

LANES = 128
WIDE = 2048
BATCH = 4096
LOAD = 512
VMEM_MIB = 60


def sylvester(order):
    table = np.ones((1, 1), np.float32)
    base = np.array([[1.0, 1.0], [1.0, -1.0]], np.float32)
    while table.shape[0] < order:
        table = np.kron(table, base)
    return table


def halves(value):
    high = value.astype(jnp.bfloat16)
    low = (value - high.astype(jnp.float32)).astype(jnp.bfloat16)
    return high, low


def sampled_gradient(place_ref, index_ref, near_act_ref, far_act_ref, far_ref, table_ref, small_ref, near_ref, *refs):
    grd_refs, (out_ref, mixed, stage, signs, tokens, act, rows_v, rows_s, sem) = refs[:-9], refs[-9:]
    rows = act.shape[0]
    outer = mixed.shape[0] // rows
    width = outer * LANES
    piece, last = pl.program_id(0), pl.num_programs(0) - 1
    here, core = lax.div(place_ref[0], 2), lax.rem(place_ref[0], 2)
    row_copy = pltpu.make_async_copy(rows_v, rows_s, sem)

    @pl.when(piece == 0)
    def _():
        index = index_ref[...]
        row = (index // width) % rows
        rows_v[...] = (index % width) // LANES * rows + row
        row_copy.start()
        chips = len(grd_refs) // 2
        depth = grd_refs[0].shape[0]
        for which in range(2):
            for j in range(chips):
                source = lax.rem(here + j, chips) * (2 * depth) + lax.rem(core + which, 2) * depth
                source = pl.ds(pl.multiple_of(source, depth), depth)
                target = pl.ds((which * chips + j) * depth, depth)
                tokens[target, :rows // 2] = near_act_ref[core, source, :]
                tokens[target, rows // 2:] = far_act_ref[core, source, :]
        act[...] = tokens[...].T

    grd = jnp.concatenate([ref[...] for ref in grd_refs], axis=0)
    value = jnp.dot(act[...], grd, preferred_element_type=jnp.float32)
    near, far = value[: rows // 2], value[rows // 2:]
    columns = pl.ds(pl.multiple_of(piece * WIDE, WIDE), WIDE)
    near = jnp.where(near_ref[...] == 1, near, -near)
    far = jnp.where(far_ref[:, columns] == 1, far, -far)
    parts = [part for half in zip(halves(near), halves(far)) for part in half]
    out = jnp.dot(table_ref[core], jnp.concatenate(parts, axis=0), preferred_element_type=jnp.float32)
    for t in range(WIDE // LANES):
        first = pl.multiple_of((piece * (WIDE // LANES) + t) * rows, rows)
        mixed[pl.ds(first, rows), :] = out[:, t * LANES:(t + 1) * LANES]

    @pl.when(piece == last)
    def _():
        def outer_step(i, carry):
            first = pl.multiple_of(i * 8, 8)
            tiles = [mixed[pl.ds(pl.multiple_of(m * rows + first, 8), 8), :] for m in range(outer)]
            step = 1
            while step < outer:
                tiles = [tiles[m ^ step] - tiles[m] if m & step else tiles[m] + tiles[m ^ step] for m in range(outer)]
                step *= 2
            for m in range(outer):
                mixed[pl.ds(pl.multiple_of(m * rows + first, 8), 8), :] = tiles[m]
            return carry

        lax.fori_loop(0, rows // 8, outer_step, 0)

        row_copy.wait()

        across = lax.broadcasted_iota(jnp.int32, (LANES, LANES), 1)
        diagonal = lax.broadcasted_iota(jnp.int32, (LANES, LANES), 0) == across
        ones = jnp.ones((2 * LANES, LANES), jnp.bfloat16)

        def load_step(i, carry):
            first = pl.multiple_of(i * LOAD, LOAD)
            group = pl.ds(pl.multiple_of(i * (LOAD // LANES), LOAD // LANES), LOAD // LANES)
            inner = (index_ref[group, :] % LANES).astype(jnp.float32)
            spread = [jnp.where(diagonal, inner[g:g + 1, :], 0.0).astype(jnp.bfloat16) for g in range(LOAD // LANES)]
            spread = jnp.dot(jnp.concatenate(spread, axis=0), ones[:LANES], preferred_element_type=jnp.float32)
            lane = lax.broadcasted_iota(jnp.int32, (LOAD, LANES), 1).astype(jnp.float32)
            chosen = jnp.where(spread == lane, 1.0, 0.0).astype(jnp.bfloat16)
            pattern = jnp.dot(chosen, small_ref[...], preferred_element_type=jnp.float32)
            signs[pl.ds(first, LOAD), :] = pattern.astype(jnp.bfloat16)
            for s in range(LOAD):
                stage[pl.ds(first + s, 1), :] = mixed[pl.ds(rows_s[i * (LOAD // LANES) + s // LANES, s % LANES], 1), :]
            return carry

        lax.fori_loop(0, stage.shape[0] // LOAD, load_step, 0)

        def inner_step(i, carry):
            batch = pl.ds(pl.multiple_of(i * BATCH, BATCH), BATCH)
            terms = jnp.concatenate(halves(stage[batch, :] * signs[batch, :].astype(jnp.float32)), axis=1)
            total = jnp.dot(terms, ones, preferred_element_type=jnp.float32)
            lines = BATCH // LANES
            sums = [jnp.sum(jnp.where(diagonal, total[g * LANES:(g + 1) * LANES], 0.0), axis=0, keepdims=True) for g in range(lines)]
            out_ref[pl.ds(pl.multiple_of(i * lines, lines), lines), :] = jnp.concatenate(sums, axis=0)
            return carry

        lax.fori_loop(0, stage.shape[0] // BATCH, inner_step, 0)


def local_samples(near_act, far_act, blocks, near, far, place, sample_index):
    tokens = near_act.shape[1]
    rows = 2 * near_act.shape[2]
    width = near.shape[1]
    count = sample_index.shape[0]
    full = sylvester(rows)
    left, right = full[:, : rows // 2], full[:, rows // 2:]
    tables = np.stack([np.concatenate(pair, axis=1) for pair in ((left, right, left, right), (right, left, right, left))])
    vmem = pl.BlockSpec(memory_space=pltpu.VMEM)
    return pl.pallas_call(
        sampled_gradient,
        grid=(width // WIDE,),
        out_shape=jax.ShapeDtypeStruct((count // LANES, LANES), jnp.float32),
        in_specs=[pl.BlockSpec(memory_space=pltpu.SMEM)]
        + [vmem] * 6
        + [pl.BlockSpec((part.shape[0], WIDE), lambda i: (0, i)) for part in (near, *blocks)],
        out_specs=pl.BlockSpec((count // LANES, LANES), lambda i: (0, 0)),
        scratch_shapes=[
            pltpu.VMEM((rows * width // LANES, LANES), jnp.float32),
            pltpu.VMEM((count, LANES), jnp.float32),
            pltpu.VMEM((count, LANES), jnp.bfloat16),
            pltpu.VMEM((tokens, rows), jnp.bfloat16),
            pltpu.VMEM((rows, tokens), jnp.bfloat16),
            pltpu.VMEM((count // LANES, LANES), jnp.int32),
            pltpu.SMEM((count // LANES, LANES), jnp.int32),
            pltpu.SemaphoreType.DMA,
        ],
        compiler_params=pltpu.CompilerParams(vmem_limit_bytes=VMEM_MIB * 1024 * 1024),
        name="sampled_gradient",
    )(
        place[None],
        sample_index.reshape(count // LANES, LANES),
        near_act,
        far_act,
        far,
        jnp.asarray(tables, jnp.bfloat16),
        jnp.asarray(sylvester(LANES), jnp.bfloat16),
        near,
        *blocks,
    )


def around(blocks, axis):
    size = lax.axis_size(axis)
    up = [(i, (i + 1) % size) for i in range(size)]
    down = [(i, (i - 1) % size) for i in range(size)]
    ups, downs = [[[block] for block in blocks] for _ in range(2)]
    for step in range(size // 2):
        for chain in ups:
            chain.append(lax.ppermute(chain[-1], axis, up))
        if step < (size - 1) // 2:
            for chain in downs:
                chain.append(lax.ppermute(chain[-1], axis, down))
    return [part for one, two in zip(downs, ups) for part in one + two[:0:-1]]


def to_all(value, axes):
    size = lax.axis_size(axes)
    return lax.all_to_all(jnp.broadcast_to(value[None], (size,) + value.shape), axes, 0, 0, tiled=True)


def per_device(activations, out_grad, sign_bits, sample_index):
    seq_len, width = activations.shape[1], out_grad.shape[2]
    chips = lax.axis_size("z")
    here, core = lax.axis_index("z"), lax.axis_index("core")
    swap = [(0, 1), (1, 0)]

    mine = lax.dynamic_index_in_dim(out_grad, core, 0, keepdims=False)
    other = lax.ppermute(lax.dynamic_index_in_dim(out_grad, 1 - core, 0, keepdims=False), "core", swap)
    far_act = lax.ppermute(activations, "core", swap)
    far = lax.ppermute(sign_bits, "core", swap)
    blocks = around([mine, other], "z")

    terms = local_samples(activations, far_act, blocks, sign_bits, far, lax.axis_index(("z", "core")), sample_index)
    feature_count = sample_index.shape[0]
    per = feature_count // (2 * chips)
    terms = lax.all_to_all(terms.reshape(2 * chips, per), ("z", "core"), 0, 0, tiled=True)
    signs = lax.dynamic_index_in_dim(jnp.asarray(sylvester(chips), jnp.float32), here, 0, keepdims=False)
    scale = 1.0 / (width * float(seq_len) ** 0.5)
    features = jnp.sum(terms.reshape(chips, 2, per) * signs[:, None, None], axis=0) * scale
    everyone = to_all(features, "ex").reshape(-1, per)
    inner = jnp.dot(features, everyone.T, precision=lax.Precision.HIGHEST)
    gram = jnp.sum(to_all(inner, ("z", "core")), axis=0) / feature_count
    return (features, gram)


def solution(mesh):
    params, groups = mesh.devices.shape
    chips = Mesh(mesh.devices.reshape(params // 2, 2, groups), ("z", "core", "ex"))
    param = ("z", "core")
    return jax.shard_map(
        per_device,
        mesh=chips,
        in_specs=(P("ex", None, param), P("ex", param, None), P(param, None), P()),
        out_specs=(P("ex", param), P("ex", None)),
        check_vma=False,
    )
```

```python
import jax
import jax.numpy as jnp
import numpy as np
from jax import lax
from jax.experimental import pallas as pl
from jax.experimental.pallas import tpu as pltpu
from jax.sharding import Mesh, PartitionSpec as P

LANES = 128
WIDE = 2048
BATCH = 4096
LOAD = 512
VMEM_MIB = 60


def sylvester(order):
    table = np.ones((1, 1), np.float32)
    base = np.array([[1.0, 1.0], [1.0, -1.0]], np.float32)
    while table.shape[0] < order:
        table = np.kron(table, base)
    return table


def halves(value):
    high = value.astype(jnp.bfloat16)
    low = (value - high.astype(jnp.float32)).astype(jnp.bfloat16)
    return high, low


def sampled_gradient(place_ref, index_ref, near_act_ref, far_act_ref, far_ref, table_ref, small_ref, near_ref, *refs):
    grd_refs, (out_ref, mixed, stage, signs, tokens, act, rows_v, rows_s, sem) = refs[:-9], refs[-9:]
    rows = act.shape[0]
    outer = mixed.shape[0] // rows
    width = outer * LANES
    piece, last = pl.program_id(0), pl.num_programs(0) - 1
    here, core = lax.div(place_ref[0], 2), lax.rem(place_ref[0], 2)
    row_copy = pltpu.make_async_copy(rows_v, rows_s, sem)

    @pl.when(piece == 0)
    def _():
        index = index_ref[...]
        row = (index // width) % rows
        rows_v[...] = (index % width) // LANES * rows + row
        row_copy.start()
        chips = len(grd_refs) // 2
        depth = grd_refs[0].shape[0]
        for which in range(2):
            for j in range(chips):
                source = lax.rem(here + j, chips) * (2 * depth) + lax.rem(core + which, 2) * depth
                source = pl.ds(pl.multiple_of(source, depth), depth)
                target = pl.ds((which * chips + j) * depth, depth)
                tokens[target, :rows // 2] = near_act_ref[core, source, :]
                tokens[target, rows // 2:] = far_act_ref[core, source, :]
        act[...] = tokens[...].T

    grd = jnp.concatenate([ref[...] for ref in grd_refs], axis=0)
    value = jnp.dot(act[...], grd, preferred_element_type=jnp.float32)
    near, far = value[: rows // 2], value[rows // 2:]
    columns = pl.ds(pl.multiple_of(piece * WIDE, WIDE), WIDE)
    near = near * near_ref[...].astype(jnp.float32)
    far = far * far_ref[:, columns].astype(jnp.float32)
    parts = [part for half in zip(halves(near), halves(far)) for part in half]
    out = jnp.dot(table_ref[core], jnp.concatenate(parts, axis=0), preferred_element_type=jnp.float32)
    for t in range(WIDE // LANES):
        first = pl.multiple_of((piece * (WIDE // LANES) + t) * rows, rows)
        mixed[pl.ds(first, rows), :] = out[:, t * LANES:(t + 1) * LANES]

    @pl.when(piece == last)
    def _():
        def outer_step(i, carry):
            first = pl.multiple_of(i * 8, 8)
            tiles = [mixed[pl.ds(pl.multiple_of(m * rows + first, 8), 8), :] for m in range(outer)]
            step = 1
            while step < outer:
                tiles = [tiles[m ^ step] - tiles[m] if m & step else tiles[m] + tiles[m ^ step] for m in range(outer)]
                step *= 2
            for m in range(outer):
                mixed[pl.ds(pl.multiple_of(m * rows + first, 8), 8), :] = tiles[m]
            return carry

        lax.fori_loop(0, rows // 8, outer_step, 0)

        row_copy.wait()

        across = lax.broadcasted_iota(jnp.int32, (LANES, LANES), 1)
        diagonal = lax.broadcasted_iota(jnp.int32, (LANES, LANES), 0) == across
        ones = jnp.ones((2 * LANES, LANES), jnp.bfloat16)

        def load_step(i, carry):
            first = pl.multiple_of(i * LOAD, LOAD)
            group = pl.ds(pl.multiple_of(i * (LOAD // LANES), LOAD // LANES), LOAD // LANES)
            inner = (index_ref[group, :] % LANES).astype(jnp.float32)
            spread = [jnp.where(diagonal, inner[g:g + 1, :], 0.0).astype(jnp.bfloat16) for g in range(LOAD // LANES)]
            spread = jnp.dot(jnp.concatenate(spread, axis=0), ones[:LANES], preferred_element_type=jnp.float32)
            lane = lax.broadcasted_iota(jnp.int32, (LOAD, LANES), 1).astype(jnp.float32)
            chosen = jnp.where(spread == lane, 1.0, 0.0).astype(jnp.bfloat16)
            pattern = jnp.dot(chosen, small_ref[...], preferred_element_type=jnp.float32)
            signs[pl.ds(first, LOAD), :] = pattern.astype(jnp.bfloat16)
            for s in range(LOAD):
                stage[pl.ds(first + s, 1), :] = mixed[pl.ds(rows_s[i * (LOAD // LANES) + s // LANES, s % LANES], 1), :]
            return carry

        lax.fori_loop(0, stage.shape[0] // LOAD, load_step, 0)

        def inner_step(i, carry):
            batch = pl.ds(pl.multiple_of(i * BATCH, BATCH), BATCH)
            terms = jnp.concatenate(halves(stage[batch, :] * signs[batch, :].astype(jnp.float32)), axis=1)
            total = jnp.dot(terms, ones, preferred_element_type=jnp.float32)
            lines = BATCH // LANES
            sums = [jnp.sum(jnp.where(diagonal, total[g * LANES:(g + 1) * LANES], 0.0), axis=0, keepdims=True) for g in range(lines)]
            out_ref[pl.ds(pl.multiple_of(i * lines, lines), lines), :] = jnp.concatenate(sums, axis=0)
            return carry

        lax.fori_loop(0, stage.shape[0] // BATCH, inner_step, 0)


def local_samples(near_act, far_act, blocks, near, far, place, sample_index):
    tokens = near_act.shape[1]
    rows = 2 * near_act.shape[2]
    width = near.shape[1]
    count = sample_index.shape[0]
    full = sylvester(rows)
    left, right = full[:, : rows // 2], full[:, rows // 2:]
    tables = np.stack([np.concatenate(pair, axis=1) for pair in ((left, right, left, right), (right, left, right, left))])
    vmem = pl.BlockSpec(memory_space=pltpu.VMEM)
    return pl.pallas_call(
        sampled_gradient,
        grid=(width // WIDE,),
        out_shape=jax.ShapeDtypeStruct((count // LANES, LANES), jnp.float32),
        in_specs=[pl.BlockSpec(memory_space=pltpu.SMEM)]
        + [vmem] * 6
        + [pl.BlockSpec((part.shape[0], WIDE), lambda i: (0, i)) for part in (near, *blocks)],
        out_specs=pl.BlockSpec((count // LANES, LANES), lambda i: (0, 0)),
        scratch_shapes=[
            pltpu.VMEM((rows * width // LANES, LANES), jnp.float32),
            pltpu.VMEM((count, LANES), jnp.float32),
            pltpu.VMEM((count, LANES), jnp.bfloat16),
            pltpu.VMEM((tokens, rows), jnp.bfloat16),
            pltpu.VMEM((rows, tokens), jnp.bfloat16),
            pltpu.VMEM((count // LANES, LANES), jnp.int32),
            pltpu.SMEM((count // LANES, LANES), jnp.int32),
            pltpu.SemaphoreType.DMA,
        ],
        compiler_params=pltpu.CompilerParams(vmem_limit_bytes=VMEM_MIB * 1024 * 1024),
        name="sampled_gradient",
    )(
        place[None],
        sample_index.reshape(count // LANES, LANES),
        near_act,
        far_act,
        far,
        jnp.asarray(tables, jnp.bfloat16),
        jnp.asarray(sylvester(LANES), jnp.bfloat16),
        near,
        *blocks,
    )


def around(blocks, axis):
    size = lax.axis_size(axis)
    up = [(i, (i + 1) % size) for i in range(size)]
    down = [(i, (i - 1) % size) for i in range(size)]
    ups, downs = [[[block] for block in blocks] for _ in range(2)]
    for _ in range(size // 2 - 1):
        for chain in ups:
            chain.append(lax.ppermute(chain[-1], axis, up))
        for chain in downs:
            chain.append(lax.ppermute(chain[-1], axis, down))
    ups[0].append(lax.ppermute(ups[0][-1], axis, up))
    downs[1].append(lax.ppermute(downs[1][-1], axis, down))
    return [part for one, two in zip(downs, ups) for part in one + two[:0:-1]]


def to_all(value, axes):
    size = lax.axis_size(axes)
    return lax.all_to_all(jnp.broadcast_to(value[None], (size,) + value.shape), axes, 0, 0, tiled=True)


def per_device(activations, out_grad, sign_bits, sample_index):
    seq_len, width = activations.shape[1], out_grad.shape[2]
    chips = lax.axis_size("z")
    here, core = lax.axis_index("z"), lax.axis_index("core")
    swap = [(0, 1), (1, 0)]

    mine = lax.dynamic_index_in_dim(out_grad, core, 0, keepdims=False)
    other = lax.ppermute(lax.dynamic_index_in_dim(out_grad, 1 - core, 0, keepdims=False), "core", swap)
    far_act = lax.ppermute(activations, "core", swap)
    near = jnp.where(sign_bits == 1, 1.0, -1.0).astype(jnp.bfloat16)
    far = lax.ppermute(near, "core", swap)
    blocks = around([mine, other], "z")

    terms = local_samples(activations, far_act, blocks, near, far, lax.axis_index(("z", "core")), sample_index)
    feature_count = sample_index.shape[0]
    per = feature_count // (2 * chips)
    terms = lax.all_to_all(terms.reshape(2 * chips, per), ("z", "core"), 0, 0, tiled=True)
    signs = lax.dynamic_index_in_dim(jnp.asarray(sylvester(chips), jnp.float32), here, 0, keepdims=False)
    scale = 1.0 / (width * float(seq_len) ** 0.5)
    features = jnp.sum(terms.reshape(chips, 2, per) * signs[:, None, None], axis=0) * scale
    everyone = to_all(features, "ex").reshape(-1, per)
    inner = jnp.dot(features, everyone.T, precision=lax.Precision.HIGHEST)
    gram = jnp.sum(to_all(inner, ("z", "core")), axis=0) / feature_count
    return (features, gram)


def solution(mesh):
    params, groups = mesh.devices.shape
    chips = Mesh(mesh.devices.reshape(params // 2, 2, groups), ("z", "core", "ex"))
    param = ("z", "core")
    return jax.shard_map(
        per_device,
        mesh=chips,
        in_specs=(P("ex", None, param), P("ex", param, None), P(param, None), P()),
        out_specs=(P("ex", param), P("ex", None)),
        check_vma=False,
    )
```
